32 devices in a mesh: lat: 2 (over x), lon: 16 (over z, y, core).
Axes of the slice: x: 2, y: 2, z: 4, core: 2. Of those that a mesh axis runs over, the one named last changes fastest.
Arguments:
- stream: bfloat16 [2, 48, 48, 768], P(None, 'lat', 'lon'), may hold values from -6 to 6
- land: int32 [48, 48], P('lat', 'lon'), may hold values from 0 to 16
- orography: int32 [48, 48], P('lat', 'lon'), may hold values from 0 to 7
- land_vector: float32 [768], replicated, may hold values from -6 to 6
- orography_table: float32 [8, 768], replicated, may hold values from -6 to 6
- gain_one: float32 [768], replicated, may hold values from 0.1 to 1.9
- qkv_one: bfloat16 [768, 2304], replicated, may hold values from -0.21875 to 0.21875
- proj_one: bfloat16 [768, 768], replicated, may hold values from -0.875 to 0.875
- table_one: bfloat16 [4, 12, 6336], P('lat'), may hold values from -4 to 250
- gain_two: float32 [768], replicated, may hold values from 0.1 to 1.9
- qkv_two: bfloat16 [768, 2304], replicated, may hold values from -0.21875 to 0.21875
- proj_two: bfloat16 [768, 768], replicated, may hold values from -0.875 to 0.875
- table_two: bfloat16 [4, 12, 6336], P('lat'), may hold values from -4 to 250
- cotangent: bfloat16 [2, 48, 48, 768], P(None, 'lat', 'lon'), may hold values from -6 to 6
Outputs:
- output: bfloat16 [2, 48, 48, 768], P(None, 'lat', 'lon')
- grad_stream: bfloat16 [2, 48, 48, 768], P(None, 'lat', 'lon')
The draws below stay inside these ranges and needn't reach their ends.
All inputs are finite; a program needn't handle non-finite values.
Results may differ from the reference program's by a relative error of at most 0.027.
Values may be sent and summed in bfloat16 or wider, within the bound.
A program may use at most 192 MiB of HBM per device.

```python
import jax
import jax.numpy as jnp
from jax import lax

D = 768
HEADS = 12
WZ = 2
WLAT = 12
WLON = 6
LAT = 48
LON = 48
TYPES = 4
TABLE = 6336
OROG = 8
LAND = 16


def draw_table_one(key, part):
    key = jax.random.fold_in(key, 11)
    shape = (TYPES, HEADS, TABLE)
    return jnp.clip(jax.random.normal(key, shape, jnp.float32), -4.0, 4.0).astype(jnp.bfloat16)


def draw_table_two(key, part):
    key = jax.random.fold_in(key, 23)
    shape = (TYPES, HEADS, TABLE)
    return jnp.clip(jax.random.normal(key, shape, jnp.float32), -4.0, 4.0).astype(jnp.bfloat16)


def touch_ends(entries, rng, smallest, high):
    index_at = [jax.random.randint(jax.random.fold_in(rng, axis), (), 0, length) for axis, length in enumerate(entries.shape)]
    main_axis = entries.shape.index(max(entries.shape))
    beside = index_at[:main_axis] + [(index_at[main_axis] + 1) % entries.shape[main_axis]] + index_at[main_axis + 1:]
    return entries.at[tuple(index_at)].set(smallest).at[tuple(beside)].set(high)


def shard_levels(stream_key, extent, cuts, least, top_value):
    level = 1.0
    for dim, blocks in cuts:
        draws = jax.random.uniform(jax.random.fold_in(jax.random.fold_in(stream_key, 6), dim), (blocks,), jnp.float32, least / len(cuts), top_value / len(cuts))
        level = level * jnp.repeat(jnp.exp(draws), extent[dim] // blocks).reshape((-1,) + (1,) * (len(extent) - 1 - dim))
    return level


def normal_values(key, shape, deviation, limit, cuts=(), kind=jnp.bfloat16):
    values = deviation * jax.random.normal(key, shape, jnp.float32)
    if cuts:
        values = values * shard_levels(key, shape, cuts, -0.22, 0.18)
    return jnp.clip(values, -limit, limit).astype(kind)


def setup_inputs(seed: int = 0) -> dict:
    key_list = jax.random.split(jax.random.key(seed), 15)
    return {
        "stream": normal_values(key_list[0], (WZ, LAT, LON, D), 1.0, 6.0, ((1, 2), (2, 16))),
        "land": touch_ends(jax.random.randint(key_list[1], (LAT, LON), 0, LAND + 1), jax.random.fold_in(key_list[1], 1), 0, LAND).astype(jnp.int32),
        "orography": touch_ends(jax.random.randint(key_list[2], (LAT, LON), 0, OROG), jax.random.fold_in(key_list[2], 1), 0, OROG - 1).astype(jnp.int32),
        "land_vector": normal_values(key_list[3], (D,), 1.0, 6.0, (), jnp.float32),
        "orography_table": normal_values(key_list[4], (OROG, D), 1.0, 6.0, (), jnp.float32),
        "gain_one": jnp.clip(1.0 + 0.18 * jax.random.normal(key_list[5], (D,), jnp.float32), 0.1, 1.9),
        "qkv_one": normal_values(key_list[6], (D, 3 * D), D ** -0.5, 0.21875),
        "proj_one": normal_values(key_list[7], (D, D), (D // 16) ** -0.5, 0.875),
        "table_one": draw_table_one(jax.random.fold_in(key_list[14], 71), 0),
        "gain_two": jnp.clip(1.0 + 0.18 * jax.random.normal(key_list[9], (D,), jnp.float32), 0.1, 1.9),
        "qkv_two": normal_values(key_list[10], (D, 3 * D), D ** -0.5, 0.21875),
        "proj_two": normal_values(key_list[11], (D, D), (D // 16) ** -0.5, 0.875),
        "table_two": draw_table_two(jax.random.fold_in(key_list[14], 71), 0),
        "cotangent": normal_values(key_list[13], (WZ, LAT, LON, D), 1.0, 6.0, ((1, 2), (2, 16))),
    }


epsilon = 1e-05
highest = lax.Precision.HIGHEST

def layer_norm(stream, gain):
    values = stream.astype(jnp.float32)
    average = lax.optimization_barrier(jnp.mean(values, axis=-1, keepdims=True))
    centred = values - average
    inverse = lax.rsqrt(lax.optimization_barrier(jnp.mean(centred * centred, axis=-1, keepdims=True)) + epsilon)
    normed = centred * inverse
    return ((normed * gain).astype(jnp.bfloat16), normed, inverse)

def norm_back(grad_normed_in, normed, inverse, gain):
    scaled = grad_normed_in * gain
    first = lax.optimization_barrier(jnp.mean(scaled, axis=-1, keepdims=True))
    second = lax.optimization_barrier(jnp.mean(scaled * normed, axis=-1, keepdims=True))
    return (scaled - first - normed * second) * inverse

def window_bias(table):
    heads = table.shape[0]
    shaped = table.astype(jnp.float32).reshape(heads, WZ, WZ, WLAT, WLAT, 2 * WLON - 1)
    column = jnp.arange(WLON, dtype=jnp.int32)
    offset = column[:, None] - column[None, :] + (WLON - 1)
    picked = jnp.take(shaped, offset, axis=5)
    picked = picked.transpose(0, 1, 3, 5, 2, 4, 6)
    return picked.reshape(heads, WZ, WLAT, WLON, WZ * WLAT * WLON)

def split_windows(array):
    levels, rows, width, chans = array.shape
    shaped = array.reshape(levels, rows // WLAT, WLAT, width, chans).transpose(1, 0, 2, 3, 4)
    return shaped.reshape(rows // WLAT, levels * WLAT * width, chans)

def join_windows(array, levels, width):
    windows = array.shape[0]
    chans = array.shape[-1]
    shaped = array.reshape(windows, levels, WLAT, width, chans).transpose(1, 0, 2, 3, 4)
    return shaped.reshape(levels, windows * WLAT, width, chans)

def pair_mask(row_start, rows, total_rows, width):
    line = row_start + jnp.arange(rows, dtype=jnp.int32)
    upper = (line >= total_rows - WLAT // 2).reshape(rows // WLAT, 1, WLAT, 1)
    query_side = jnp.broadcast_to(upper, (rows // WLAT, WZ, WLAT, width)).reshape(rows // WLAT, -1)
    key_side = jnp.broadcast_to(upper, (rows // WLAT, WZ, WLAT, 2 * width)).reshape(rows // WLAT, -1)
    return query_side[:, :, None] == key_side[:, None, :]

def attend(queries, keys, values, bias, allowed):
    scale = queries.shape[-1] ** (-0.5)
    scores = jnp.einsum('wqhe,wkhe->whqk', queries.astype(jnp.float32), keys.astype(jnp.float32), precision=highest) * scale + bias
    if allowed is not None:
        scores = jnp.where(allowed[:, None], scores, -1000000000.0)
    largest = lax.optimization_barrier(jnp.max(scores, axis=-1, keepdims=True))
    expo = jnp.exp(scores - largest)
    probs = expo / lax.optimization_barrier(jnp.sum(expo, axis=-1, keepdims=True))
    rounded = lax.optimization_barrier(probs.astype(jnp.bfloat16)).astype(jnp.float32)
    mixed = jnp.einsum('whqk,wkhe->wqhe', rounded, values.astype(jnp.float32), precision=highest)
    return (mixed.astype(jnp.bfloat16), probs)

def attend_back(queries, keys, values, probs, grad_mixed):
    scale = queries.shape[-1] ** (-0.5)
    rounded = lax.optimization_barrier(probs.astype(jnp.bfloat16)).astype(jnp.float32)
    grad_wide = grad_mixed.astype(jnp.float32)
    grad_probs = jnp.einsum('wqhe,wkhe->whqk', grad_wide, values.astype(jnp.float32), precision=highest)
    inner = lax.optimization_barrier(jnp.sum(probs * grad_probs, axis=-1, keepdims=True))
    grad_scores = probs * (grad_probs - inner) * scale
    grad_scores = lax.optimization_barrier(grad_scores.astype(jnp.bfloat16)).astype(jnp.float32)
    grad_q = jnp.einsum('whqk,wkhe->wqhe', grad_scores, keys.astype(jnp.float32), precision=highest)
    grad_k = jnp.einsum('whqk,wqhe->wkhe', grad_scores, queries.astype(jnp.float32), precision=highest)
    grad_v = jnp.einsum('whqk,wqhe->wkhe', rounded, grad_wide, precision=highest)
    return (grad_q, grad_k.astype(jnp.bfloat16), grad_v.astype(jnp.bfloat16))

def column_forward(column, gain, weight_qkv, weight_proj, biases, allowed):
    levels, rows, width, dims = column.shape
    heads = biases.shape[1]
    depth = dims // heads
    windows = rows // WLAT
    half = width // 2
    normed_in, normed, inverse = layer_norm(column, gain)
    projected = jnp.dot(normed_in.reshape(-1, dims), weight_qkv, preferred_element_type=jnp.float32)
    projected = projected.astype(jnp.bfloat16).reshape(levels, rows, width, 3 * dims)
    key_values = split_windows(projected[..., dims:])
    keys = key_values[..., :dims].reshape(windows, -1, heads, depth)
    values = key_values[..., dims:].reshape(windows, -1, heads, depth)
    pieces = []
    saved = []
    for side in range(2):
        queries = split_windows(projected[:, :, side * half:(side + 1) * half, :dims]).reshape(windows, -1, heads, depth)
        bias = biases[:, :, :, :, side * half:(side + 1) * half].reshape(windows, heads, -1, biases.shape[-1])
        mixed, probs = attend(queries, keys, values, bias, allowed)
        pieces.append(join_windows(mixed.reshape(windows, -1, dims), levels, half))
        saved.append((queries, probs))
    mixed_all = jnp.concatenate(pieces, axis=2)
    added = jnp.dot(mixed_all.reshape(-1, dims), weight_proj, preferred_element_type=jnp.float32).reshape(column.shape)
    result = (column.astype(jnp.float32) + added).astype(jnp.bfloat16)
    return (result, (normed, inverse, keys, values, saved))

def column_backward(column, grad, gain, weight_qkv, weight_proj, biases, allowed):
    result, (normed, inverse, keys, values, saved) = column_forward(column, gain, weight_qkv, weight_proj, biases, allowed)
    levels, rows, width, dims = column.shape
    heads = biases.shape[1]
    depth = dims // heads
    windows = rows // WLAT
    half = width // 2
    grad_mixed = jnp.dot(grad.reshape(-1, dims), weight_proj.T, preferred_element_type=jnp.float32)
    grad_mixed = grad_mixed.astype(jnp.bfloat16).reshape(grad.shape)
    query_parts = []
    key_total = jnp.zeros((windows, WZ * WLAT * width, heads, depth), jnp.float32)
    value_total = jnp.zeros((windows, WZ * WLAT * width, heads, depth), jnp.float32)
    for side in range(2):
        queries, probs = saved[side]
        grad_part = split_windows(grad_mixed[:, :, side * half:(side + 1) * half]).reshape(windows, -1, heads, depth)
        grad_q, grad_k, grad_v = attend_back(queries, keys, values, probs, grad_part)
        query_parts.append(join_windows(grad_q.reshape(windows, -1, dims), levels, half))
        key_total = key_total + grad_k.astype(jnp.float32)
        value_total = value_total + grad_v.astype(jnp.float32)
    query_grads = jnp.concatenate(query_parts, axis=2).astype(jnp.bfloat16)
    both = jnp.concatenate([key_total.reshape(windows, -1, dims), value_total.reshape(windows, -1, dims)], axis=-1)
    key_grads = join_windows(both.astype(jnp.bfloat16), levels, width)
    grad_qkv = jnp.concatenate([query_grads, key_grads], axis=-1)
    grad_normed_in = jnp.dot(grad_qkv.reshape(-1, 3 * dims), weight_qkv.T, preferred_element_type=jnp.float32).reshape(grad.shape)
    return (grad.astype(jnp.float32) + norm_back(grad_normed_in, normed, inverse, gain)).astype(jnp.bfloat16)

def run_block(field, gain, weight_qkv, weight_proj, table, allowed, grad):
    levels, rows, width, dims = field.shape
    columns = width // WLON
    biases = jax.vmap(window_bias)(table)
    pieces = field.reshape(levels, rows, columns, WLON, dims).transpose(2, 0, 1, 3, 4)
    if grad is None:

        def forward_one(column):
            return column_forward(column, gain, weight_qkv, weight_proj, biases, allowed)[0]
        done = lax.map(forward_one, pieces)
    else:
        grad_pieces = grad.reshape(levels, rows, columns, WLON, dims).transpose(2, 0, 1, 3, 4)

        def backward_one(pair):
            return column_backward(pair[0], pair[1], gain, weight_qkv, weight_proj, biases, allowed)
        done = lax.map(backward_one, (pieces, grad_pieces))
    return done.transpose(1, 2, 0, 3, 4).reshape(field.shape)

def reference(stream, land, orography, land_vector, orography_table, gain_one, qkv_one, proj_one, table_one, gain_two, qkv_two, proj_two, table_two, cotangent):
    dims = stream.shape[-1]
    onehot = (orography[..., None] == jnp.arange(OROG, dtype=jnp.int32)).astype(jnp.float32)
    looked = jnp.dot(onehot.reshape(-1, OROG), orography_table, precision=highest).reshape(LAT, LON, dims)
    added = (land.astype(jnp.float32) / LAND)[..., None] * land_vector + looked
    embedded = (stream.astype(jnp.float32) + added[None]).astype(jnp.bfloat16)
    shifted = pair_mask(0, LAT, LAT, WLON // 2)
    back_shift = (-(WLAT // 2), -(WLON // 2))
    forth_shift = (WLAT // 2, WLON // 2)
    middle = run_block(embedded, gain_one, qkv_one, proj_one, table_one, None, None)
    rolled = jnp.roll(middle, back_shift, axis=(1, 2))
    turned = run_block(rolled, gain_two, qkv_two, proj_two, table_two, shifted, None)
    output = jnp.roll(turned, forth_shift, axis=(1, 2))
    grad_rolled = jnp.roll(cotangent, back_shift, axis=(1, 2))
    grad_turned = run_block(rolled, gain_two, qkv_two, proj_two, table_two, shifted, grad_rolled)
    grad_middle = jnp.roll(grad_turned, forth_shift, axis=(1, 2))
    grad_stream = run_block(embedded, gain_one, qkv_one, proj_one, table_one, None, grad_middle)
    return (output, grad_stream)
```

```python
import functools

import jax
import jax.numpy as jnp
import ml_dtypes
import numpy as np
from jax import lax
from jax.experimental import pallas as pl
from jax.experimental.pallas import tpu as pltpu
from jax.sharding import PartitionSpec as P

WZ = 2
WLAT = 12
WLON = 6
LAND = 16
HALF = WLAT // 2
WIDTH = WLON // 2
WINDOWS = 2
TOKENS = WZ * WLAT * WIDTH
SLOT = 80
ROWS = WINDOWS * SLOT
MAIN = 112
STEP = 2 * WLON - 1
RUN = WLAT * STEP
EPS = 1e-05
F32 = jnp.float32
BF16 = jnp.bfloat16
MESH = pl.DeviceIdType.MESH


def window_place(z, r, w):
    return (r // WLAT) * SLOT + w * WZ * WLAT + z * WLAT + r % WLAT


def plain_place(z, r, w):
    return (z * WINDOWS * WLAT + r) * WIDTH + w


def chunk_place(z, r, w, strip):
    chunk = r // HALF
    inner = (z * HALF + r % HALF) * WIDTH + w
    if chunk == strip:
        return MAIN + inner
    return (chunk if strip else chunk - 1) * WZ * HALF * WIDTH + inner


def permutations():
    out = np.zeros((8, ROWS, ROWS), np.float32)
    rows = WINDOWS * WLAT
    for z in range(WZ):
        for r in range(rows):
            for w in range(WIDTH):
                here = window_place(z, r, w)
                plain = plain_place(z, r, w)
                up = chunk_place(z, r, w, 0)
                down = chunk_place(z, r, w, 3)
                from_up = chunk_place(z, (r + HALF) % rows, w, 0)
                from_down = chunk_place(z, (r - HALF) % rows, w, 3)
                out[0, here, plain] = 1
                out[1, up, plain] = 1
                out[2, up, here] = 1
                out[3, here, from_up] = 1
                out[4, down, here] = 1
                out[5, here, from_down] = 1
                out[6, plain, from_down] = 1
                out[7, plain, here] = 1
    return out.astype(ml_dtypes.bfloat16)


def pickers():
    out = np.zeros((2, WZ * 256, WIDTH * 256), np.float32)
    for p in range(2):
        for w in range(WIDTH):
            for slot in range(2):
                for kw in range(WIDTH):
                    col = WIDTH * (p if slot == 0 else 1 - p) + kw
                    d = WIDTH * p + w - col + WLON - 1
                    for z in range(WZ):
                        for r in range(WLAT):
                            key = slot * SLOT + kw * WZ * WLAT + z * WLAT + r
                            out[p, z * 256 + r * STEP + d, w * 256 + key] = 1
    return out.astype(ml_dtypes.bfloat16)


def key_rows():
    out = np.zeros((8, 256), np.float32)
    for slot in range(2):
        for k in range(SLOT):
            upper = k % WLAT >= HALF
            lane = slot * SLOT + k
            if k >= TOKENS:
                out[0, lane] = -1e30
            else:
                out[1, lane] = -1e9 if upper else 0.0
                out[2, lane] = 0.0 if upper else -1e9
    return out


def land_pickers():
    rows = np.zeros((ROWS, WINDOWS * WLAT), np.float32)
    cols = np.zeros((ROWS, WIDTH), np.float32)
    for z in range(WZ):
        for r in range(WINDOWS * WLAT):
            for w in range(WIDTH):
                here = window_place(z, r, w)
                rows[here, r] = 1
                cols[here, w] = 1
    return rows.astype(ml_dtypes.bfloat16), cols


def mm(a, b):
    return lax.dot_general(a, b, (((1,), (0,)), ((), ())), preferred_element_type=F32)


def mt(a, b):
    return lax.dot_general(a, b, (((1,), (1,)), ((), ())), preferred_element_type=F32)


def tm(a, b):
    return lax.dot_general(a, b, (((0,), (0,)), ((), ())), preferred_element_type=F32)


def kernel(
    lats,
    lons,
    stream,
    land,
    orography,
    land_vector,
    orography_table,
    gain_one,
    qkv_one,
    proj_one,
    gain_two,
    qkv_two,
    proj_two,
    tables,
    cotangent,
    perms,
    picks,
    keys_row,
    land_rows,
    land_cols,
    output,
    grad_stream,
    bias,
    spread,
    probs,
    field,
    normed,
    inverse,
    qkv,
    far,
    mixed,
    back,
    grads,
    far_grads,
    got_grads,
    sent,
    got,
    send_sem,
    recv_sem,
):
    dims = stream.shape[1]
    heads = tables.shape[1] // WINDOWS
    pairs = heads // 2
    i = lax.axis_index("lat")
    j = lax.axis_index("lon")
    parity = lax.rem(j, 2)
    next_lat = lax.rem(i + 1, lats)
    prev_lat = lax.rem(i + lats - 1, lats)
    east = lax.rem(j + 1, lons)
    west = lax.rem(j + lons - 1, lons)
    partner = (i, j + 1 - 2 * parity)

    barrier = pltpu.get_barrier_semaphore()
    for peer in ((i, east), (i, west), (next_lat, east), (prev_lat, west)):
        pl.semaphore_signal(barrier, inc=1, device_id=peer, device_id_type=MESH)

    copies = []

    def send(src, dst, to):
        n = len(copies)
        copy = pltpu.make_async_remote_copy(
            src_ref=src,
            dst_ref=dst,
            send_sem=send_sem.at[n],
            recv_sem=recv_sem.at[n],
            device_id=to,
            device_id_type=MESH,
        )
        copy.start()
        copies.append(copy)
        return copy

    def roll(slot, moved, up):
        sent[slot] = moved.astype(BF16)
        main = (i, west) if up else (i, east)
        strip = (prev_lat, west) if up else (next_lat, east)
        a = send(sent.at[slot, pl.ds(0, MAIN)], got.at[slot, pl.ds(0, MAIN)], main)
        rest = pl.ds(MAIN, ROWS - MAIN)
        b = send(sent.at[slot, rest], got.at[slot, rest], strip)
        return a, b

    def arrive(both):
        for copy in both:
            copy.wait_recv()

    plain = WZ * WINDOWS * WLAT * WIDTH

    row_pick = land_rows[...]
    col_pick = land_cols[...]

    def per_token(ref):
        spread_rows = mm(row_pick, ref[...].astype(F32).astype(BF16))
        return jnp.sum(spread_rows * col_pick, axis=1, keepdims=True)

    classes = per_token(orography)
    added = (per_token(land) * (1.0 / LAND)) * land_vector[...]
    for k in range(orography_table.shape[0]):
        added = added + jnp.where(classes == float(k), 1.0, 0.0) * orography_table[k : k + 1, :]
    embedded = (mm(perms[0, :, :plain], stream[...]) + added).astype(BF16)
    field[0] = embedded

    def project(b, gain, weight):
        values = field[b].astype(F32)
        centred = values - jnp.mean(values, axis=-1, keepdims=True)
        inv = lax.rsqrt(jnp.mean(centred * centred, axis=-1, keepdims=True) + EPS)
        norm = centred * inv
        normed[b] = norm
        inverse[b] = inv
        h = (norm * gain[...]).astype(BF16)
        for part in (1, 2, 0):
            cols = slice(part * dims, (part + 1) * dims)
            qkv[b, :, cols] = mm(h, weight[:, cols]).astype(BF16)

    project(0, gain_one, qkv_one)
    pl.semaphore_wait(barrier, 4)
    kv_one = send(qkv.at[0, :, pl.ds(dims, 2 * dims)], far.at[0], partner)
    cot = roll(0, mm(perms[1, :, :plain], cotangent[...]), True)

    pick = picks[parity]
    last = jnp.where(i == lats - 1, 1.0, 0.0).astype(F32)
    pad_row = keys_row[0:1, :]
    count = WINDOWS * heads
    late = lax.broadcasted_iota(jnp.int32, (count, 256), 0) >= heads

    def expand(b):
        entries = tables[b].astype(F32)
        for za in range(WZ):
            for ra in range(WLAT):
                n = za * WLAT + ra
                for zc in range(WZ):
                    k = (za * WZ + zc) * WLAT + ra
                    spread[n * count : (n + 1) * count, zc * 256 : (zc + 1) * 256] = entries[
                        :, RUN * k : RUN * k + 256
                    ]
        for tn in range(count):
            bias[b, :, tn * SLOT + TOKENS : (tn + 1) * SLOT, :] = jnp.zeros(
                (2, SLOT - TOKENS, 128), F32
            )
        group = 4
        for first in range(0, WZ * WLAT, group):
            rows = spread[first * count : (first + group) * count, :].astype(BF16)
            for w in range(WIDTH):
                picked = mm(rows, pick[:, w * 256 : (w + 1) * 256])
                for g in range(group):
                    n = first + g
                    value = picked[g * count : (g + 1) * count, :] + pad_row
                    if b == 1:
                        forbid = keys_row[1:2, :] if n % WLAT < HALF else keys_row[2:3, :]
                        value = value + jnp.where(late, last * forbid, 0.0)
                    for half in range(2):
                        bias[b, half, pl.ds(w * WZ * WLAT + n, count, stride=SLOT), :] = value[
                            :, half * 128 : (half + 1) * 128
                        ]

    expand(0)

    low = lax.broadcasted_iota(jnp.int32, (SLOT, 128), 1) < 64
    first_half = jnp.where(low, 1.0, 0.0).astype(BF16)
    second_half = jnp.where(low, 0.0, 1.0).astype(BF16)
    scale = (dims // heads) ** -0.5

    def split(value):
        return jnp.concatenate([value * first_half, value * second_half], axis=0)

    def merge(value):
        return jnp.where(low, value[:SLOT], value[SLOT:])

    def lanes(part, pair):
        return pl.ds(pl.multiple_of(part * dims + pair * 128, 128), 128)

    def keys_of(b, rows, part, pair):
        own = qkv[b, rows, lanes(part + 1, pair)]
        other = far[b, rows, lanes(part, pair)]
        return jnp.concatenate([own, other], axis=0)

    def forward(b, t, pair, rows):
        q = split(qkv[b, rows, lanes(0, pair)])
        k = keys_of(b, rows, 0, pair)
        v = keys_of(b, rows, 1, pair)
        at = pl.multiple_of((t * heads + 2 * pair) * SLOT, SLOT)
        here = pl.ds(at, 2 * SLOT)
        offsets = jnp.concatenate([bias[b, 0, here, :], bias[b, 1, here, : 2 * SLOT - 128]], axis=1)
        scores = mt(q, k) * scale + offsets
        expo = jnp.exp(scores - jnp.max(scores, axis=-1, keepdims=True))
        p = expo * (1.0 / jnp.sum(expo, axis=-1, keepdims=True))
        rounded = p.astype(BF16)
        mixed[rows, lanes(0, pair)] = merge(mm(rounded, v)).astype(BF16)
        return q, k, v, p, rounded

    def backward(rows, pair, q, k, v, p, rounded):
        d = split(back[rows, lanes(0, pair)])
        dp = mt(d, v)
        inner = jnp.sum(p * dp, axis=-1, keepdims=True)
        ds = (p * (dp - inner) * scale).astype(BF16)
        grads[rows, lanes(0, pair)] = merge(mm(ds, k)).astype(BF16)
        dk = tm(ds, q).astype(BF16)
        dv = tm(rounded, d).astype(BF16)
        grads[rows, lanes(1, pair)] = dk[:SLOT]
        grads[rows, lanes(2, pair)] = dv[:SLOT]
        far_grads[rows, lanes(0, pair)] = dk[SLOT:]
        far_grads[rows, lanes(1, pair)] = dv[SLOT:]

    def save_at(t, pair):
        return pl.ds(pl.multiple_of((t * heads + 2 * pair) * SLOT, SLOT), 2 * SLOT)

    def finish(b, dy, gain, weight):
        dq = grads[:, :dims]
        total = mt(dq, weight[:, :dims])
        for part in (1, 2):
            cols = slice(part * dims, (part + 1) * dims)
            own = grads[:, cols].astype(F32)
            other = got_grads[b, :, (part - 1) * dims : part * dims].astype(F32)
            total = total + mt((own + other).astype(BF16), weight[:, cols])
        scaled = total * gain[...]
        norm = normed[b]
        mean = jnp.mean(scaled, axis=-1, keepdims=True)
        along = jnp.mean(scaled * norm, axis=-1, keepdims=True)
        return (dy + (scaled - mean - norm * along) * inverse[b]).astype(BF16)

    kv_one.wait_recv()

    def one(pair, carry):
        for t in range(WINDOWS):
            rows = pl.ds(t * SLOT, SLOT)
            saved = forward(0, t, pair, rows)
            probs[save_at(t, pair), :] = saved[3]
        return carry

    lax.fori_loop(0, pairs, one, 0)
    middle = (field[0].astype(F32) + mm(mixed[...], proj_one[...])).astype(BF16)
    moved = roll(1, mm(perms[2], middle), True)
    expand(1)
    arrive(moved)
    field[1] = mm(perms[3], got[1]).astype(BF16)

    project(1, gain_two, qkv_two)
    kv_two = send(qkv.at[1, :, pl.ds(dims, 2 * dims)], far.at[1], partner)
    arrive(cot)
    dy_two = mm(perms[3], got[0])
    back[...] = mt(dy_two.astype(BF16), proj_two[...]).astype(BF16)
    kv_two.wait_recv()

    def two(pair, carry):
        for t in range(WINDOWS):
            rows = pl.ds(t * SLOT, SLOT)
            backward(rows, pair, *forward(1, t, pair, rows))
        return carry

    lax.fori_loop(0, pairs, two, 0)
    dkv_two = send(far_grads, got_grads.at[1], partner)
    turned = (field[1].astype(F32) + mm(mixed[...], proj_two[...])).astype(BF16)
    result = roll(2, mm(perms[4], turned), False)
    dkv_two.wait_recv()
    grad_turned = finish(1, mm(perms[3], got[0]), gain_two, qkv_two)
    moved = roll(3, mm(perms[4], grad_turned), False)
    arrive(result)
    output[...] = mm(perms[6], got[2])[:plain].astype(BF16)
    arrive(moved)

    dy_one = mm(perms[5], got[3])
    back[...] = mt(dy_one.astype(BF16), proj_one[...]).astype(BF16)
    dkv_two.wait_send()

    def one_back(pair, carry):
        for t in range(WINDOWS):
            rows = pl.ds(t * SLOT, SLOT)
            q = split(qkv[0, rows, lanes(0, pair)])
            p = probs[save_at(t, pair), :]
            k = keys_of(0, rows, 0, pair)
            v = keys_of(0, rows, 1, pair)
            backward(rows, pair, q, k, v, p, p.astype(BF16))
        return carry

    lax.fori_loop(0, pairs, one_back, 0)
    dkv_one = send(far_grads, got_grads.at[0], partner)
    dkv_one.wait_recv()
    last_grad = finish(0, mm(perms[5], got[3]), gain_one, qkv_one)
    grad_stream[...] = mm(perms[7], last_grad)[:plain].astype(BF16)
    for copy in copies:
        if copy is not dkv_two:
            copy.wait_send()


def body(
    lats,
    lons,
    stream,
    land,
    orography,
    land_vector,
    orography_table,
    gain_one,
    qkv_one,
    proj_one,
    table_one,
    gain_two,
    qkv_two,
    proj_two,
    table_two,
    cotangent,
):
    levels, rows, width, dims = stream.shape
    types, heads, entries = table_one.shape
    plain = levels * rows * width
    tables = jnp.stack([table_one, table_two]).reshape(2, types * heads, entries)
    tables = jnp.pad(tables, ((0, 0), (0, 0), (0, 128)))
    land_rows, land_cols = land_pickers()
    wide = 3 * dims
    scratch = [
        pltpu.VMEM((2, 2, types * heads * SLOT, 128), F32),
        pltpu.VMEM((WZ * WLAT * types * heads, WZ * 256), F32),
        pltpu.VMEM((types * heads * SLOT, 2 * SLOT), F32),
        pltpu.VMEM((2, ROWS, dims), BF16),
        pltpu.VMEM((2, ROWS, dims), F32),
        pltpu.VMEM((2, ROWS, 1), F32),
        pltpu.VMEM((2, ROWS, wide), BF16),
        pltpu.VMEM((2, ROWS, 2 * dims), BF16),
        pltpu.VMEM((ROWS, dims), BF16),
        pltpu.VMEM((ROWS, dims), BF16),
        pltpu.VMEM((ROWS, wide), BF16),
        pltpu.VMEM((ROWS, 2 * dims), BF16),
        pltpu.VMEM((2, ROWS, 2 * dims), BF16),
        pltpu.VMEM((4, ROWS, dims), BF16),
        pltpu.VMEM((4, ROWS, dims), BF16),
        pltpu.SemaphoreType.DMA((12,)),
        pltpu.SemaphoreType.DMA((12,)),
    ]
    vmem = pl.BlockSpec(memory_space=pltpu.VMEM)
    out, grad = pl.pallas_call(
        functools.partial(kernel, lats, lons),
        out_shape=[jax.ShapeDtypeStruct((plain, dims), BF16)] * 2,
        in_specs=[vmem] * 18,
        out_specs=[vmem] * 2,
        scratch_shapes=scratch,
        compiler_params=pltpu.CompilerParams(
            collective_id=0, has_side_effects=True, vmem_limit_bytes=56 << 20
        ),
    )(
        stream.reshape(plain, dims),
        land,
        orography,
        land_vector.reshape(1, dims),
        orography_table,
        gain_one.reshape(1, dims),
        qkv_one,
        proj_one,
        gain_two.reshape(1, dims),
        qkv_two,
        proj_two,
        tables,
        cotangent.reshape(plain, dims),
        jnp.asarray(permutations()),
        jnp.asarray(pickers()),
        jnp.asarray(key_rows()),
        jnp.asarray(land_rows),
        jnp.asarray(land_cols),
    )
    return out.reshape(stream.shape), grad.reshape(stream.shape)


def solution(mesh):
    placed = (
        P(None, "lat", "lon", None),
        P("lat", "lon"),
        P("lat", "lon"),
        P(),
        P(),
        P(),
        P(),
        P(),
        P("lat", None, None),
        P(),
        P(),
        P(),
        P("lat", None, None),
        P(None, "lat", "lon", None),
    )
    return jax.shard_map(
        functools.partial(body, mesh.shape["lat"], mesh.shape["lon"]),
        mesh=mesh,
        in_specs=placed,
        out_specs=(P(None, "lat", "lon", None), P(None, "lat", "lon", None)),
        check_vma=False,
    )
```

```python
import functools

import jax
import jax.numpy as jnp
import ml_dtypes
import numpy as np
from jax import lax
from jax.experimental import pallas as pl
from jax.experimental.pallas import tpu as pltpu
from jax.sharding import PartitionSpec as P

WZ = 2
WLAT = 12
WLON = 6
LAND = 16
HALF = WLAT // 2
WIDTH = WLON // 2
WINDOWS = 2
TOKENS = WZ * WLAT * WIDTH
SLOT = 80
ROWS = WINDOWS * SLOT
MAIN = 112
STEP = 2 * WLON - 1
RUN = WLAT * STEP
EPS = 1e-05
F32 = jnp.float32
BF16 = jnp.bfloat16
MESH = pl.DeviceIdType.MESH


def window_place(z, r, w):
    return (r // WLAT) * SLOT + w * WZ * WLAT + z * WLAT + r % WLAT


def plain_place(z, r, w):
    return (z * WIDTH + w) * WINDOWS * WLAT + r


def chunk_place(z, r, w, strip):
    chunk = r // HALF
    inner = (z * HALF + r % HALF) * WIDTH + w
    if chunk == strip:
        return MAIN + inner
    return (chunk if strip else chunk - 1) * WZ * HALF * WIDTH + inner


def permutations():
    out = np.zeros((8, ROWS, ROWS), np.float32)
    rows = WINDOWS * WLAT
    for z in range(WZ):
        for r in range(rows):
            for w in range(WIDTH):
                here = window_place(z, r, w)
                plain = plain_place(z, r, w)
                up = chunk_place(z, r, w, 0)
                down = chunk_place(z, r, w, 3)
                from_up = chunk_place(z, (r + HALF) % rows, w, 0)
                from_down = chunk_place(z, (r - HALF) % rows, w, 3)
                out[0, here, plain] = 1
                out[1, up, plain] = 1
                out[2, up, here] = 1
                out[3, here, from_up] = 1
                out[4, down, here] = 1
                out[5, here, from_down] = 1
                out[6, plain, from_down] = 1
                out[7, plain, here] = 1
    return out.astype(ml_dtypes.bfloat16)


def pickers():
    out = np.zeros((2, WZ * 256, WIDTH * 256), np.float32)
    for p in range(2):
        for w in range(WIDTH):
            for slot in range(2):
                for kw in range(WIDTH):
                    col = WIDTH * (p if slot == 0 else 1 - p) + kw
                    d = WIDTH * p + w - col + WLON - 1
                    for z in range(WZ):
                        for r in range(WLAT):
                            key = slot * SLOT + kw * WZ * WLAT + z * WLAT + r
                            out[p, z * 256 + r * STEP + d, w * 256 + key] = 1
    return out.astype(ml_dtypes.bfloat16)


def key_rows():
    out = np.zeros((8, 256), np.float32)
    for slot in range(2):
        for k in range(SLOT):
            upper = k % WLAT >= HALF
            lane = slot * SLOT + k
            if k >= TOKENS:
                out[0, lane] = -1e30
            else:
                out[1, lane] = -1e9 if upper else 0.0
                out[2, lane] = 0.0 if upper else -1e9
    return out


def land_pickers():
    rows = np.zeros((ROWS, WINDOWS * WLAT), np.float32)
    cols = np.zeros((ROWS, WIDTH), np.float32)
    for z in range(WZ):
        for r in range(WINDOWS * WLAT):
            for w in range(WIDTH):
                here = window_place(z, r, w)
                rows[here, r] = 1
                cols[here, w] = 1
    return rows.astype(ml_dtypes.bfloat16), cols


def mm(a, b):
    return lax.dot_general(a, b, (((1,), (0,)), ((), ())), preferred_element_type=F32)


def mt(a, b):
    return lax.dot_general(a, b, (((1,), (1,)), ((), ())), preferred_element_type=F32)


def tm(a, b):
    return lax.dot_general(a, b, (((0,), (0,)), ((), ())), preferred_element_type=F32)


def kernel(
    lats,
    lons,
    stream,
    land,
    orography,
    land_vector,
    orography_table,
    gain_one,
    hbm_qkv_one,
    hbm_proj_one,
    gain_two,
    hbm_qkv_two,
    hbm_proj_two,
    table_one,
    table_two,
    cotangent,
    perms,
    hbm_picks,
    keys_row,
    land_rows,
    land_cols,
    output,
    grad_stream,
    bias,
    spread,
    entries,
    probs,
    field,
    normed,
    inverse,
    qkv,
    far,
    mixed,
    back,
    grads,
    far_grads,
    got_grads,
    sent,
    got,
    send_sem,
    recv_sem,
    qkv_one,
    proj_one,
    qkv_two,
    proj_two,
    pick,
    load_sem,
):
    dims = stream.shape[1]
    heads = table_one.shape[0]
    tables = (table_one, table_two)
    pairs = heads // 2
    i = lax.axis_index("lat")
    j = lax.axis_index("lon")
    parity = lax.rem(j, 2)
    next_lat = lax.rem(i + 1, lats)
    prev_lat = lax.rem(i + lats - 1, lats)
    east = lax.rem(j + 1, lons)
    west = lax.rem(j + lons - 1, lons)
    partner = (i, j + 1 - 2 * parity)

    loads = []
    for source, target in (
        (hbm_qkv_one, qkv_one),
        (hbm_picks.at[parity], pick),
        (hbm_proj_one, proj_one),
        (hbm_qkv_two, qkv_two),
        (hbm_proj_two, proj_two),
    ):
        load = pltpu.make_async_copy(source, target, load_sem.at[len(loads)])
        load.start()
        loads.append(load)

    barrier = pltpu.get_barrier_semaphore()
    for peer in ((i, east), (i, west), (next_lat, east), (prev_lat, west)):
        pl.semaphore_signal(barrier, inc=1, device_id=peer, device_id_type=MESH)

    copies = []

    def send(src, dst, to):
        n = len(copies)
        copy = pltpu.make_async_remote_copy(
            src_ref=src,
            dst_ref=dst,
            send_sem=send_sem.at[n],
            recv_sem=recv_sem.at[n],
            device_id=to,
            device_id_type=MESH,
        )
        copy.start()
        copies.append(copy)
        return copy

    def roll(slot, moved, up):
        sent[slot] = moved.astype(BF16)
        main = (i, west) if up else (i, east)
        strip = (prev_lat, west) if up else (next_lat, east)
        a = send(sent.at[slot, pl.ds(0, MAIN)], got.at[slot, pl.ds(0, MAIN)], main)
        rest = pl.ds(MAIN, ROWS - MAIN)
        b = send(sent.at[slot, rest], got.at[slot, rest], strip)
        return a, b

    def arrive(both):
        for copy in both:
            copy.wait_recv()

    plain = WZ * WINDOWS * WLAT * WIDTH

    row_pick = land_rows[...]
    col_pick = land_cols[...]

    def per_token(ref):
        spread_rows = mt(row_pick, ref[...].astype(F32).astype(BF16))
        return jnp.sum(spread_rows * col_pick, axis=1, keepdims=True)

    classes = per_token(orography)
    added = (per_token(land) * (1.0 / LAND)) * land_vector[...].reshape(1, dims)
    for k in range(orography_table.shape[0]):
        added = added + jnp.where(classes == float(k), 1.0, 0.0) * orography_table[k : k + 1, :]
    embedded = (mm(perms[0, :, :plain], stream[...]) + added).astype(BF16)
    field[0] = embedded

    def project(b, gain, weight):
        values = field[b].astype(F32)
        centred = values - jnp.mean(values, axis=-1, keepdims=True)
        inv = lax.rsqrt(jnp.mean(centred * centred, axis=-1, keepdims=True) + EPS)
        norm = centred * inv
        normed[b] = norm
        inverse[b] = inv
        h = (norm * gain[...].reshape(1, dims)).astype(BF16)
        loads[0 if b == 0 else 3].wait()
        for part in (1, 2):
            cols = slice(part * dims, (part + 1) * dims)
            qkv[b, :, cols] = mm(h, weight[:, cols]).astype(BF16)
        if b == 0:
            pl.semaphore_wait(barrier, 4)
        copy = send(qkv.at[b, :, pl.ds(dims, 2 * dims)], far.at[b], partner)
        qkv[b, :, :dims] = mm(h, weight[:, :dims]).astype(BF16)
        return copy

    kv_one = project(0, gain_one, qkv_one)
    cot = roll(0, mm(perms[1, :, :plain], cotangent[...]), True)

    loads[1].wait()
    last = jnp.where(i == lats - 1, 1.0, 0.0).astype(F32)
    pad_row = keys_row[0:1, :]
    count = WINDOWS * heads
    late = lax.broadcasted_iota(jnp.int32, (count, 256), 0) % WINDOWS == WINDOWS - 1

    def expand(b):
        for n in range(heads):
            entries[n * WINDOWS : (n + 1) * WINDOWS, :] = tables[b][n].astype(F32)
        for za in range(WZ):
            for ra in range(WLAT):
                n = za * WLAT + ra
                for zc in range(WZ):
                    k = (za * WZ + zc) * WLAT + ra
                    stop = min(RUN * k + 256, entries.shape[1])
                    run = entries[:, RUN * k : stop]
                    if run.shape[1] < 256:
                        rest = jnp.zeros((count, 256 - run.shape[1]), F32)
                        run = jnp.concatenate([run, rest], axis=1)
                    spread[n * count : (n + 1) * count, zc * 256 : (zc + 1) * 256] = run
        for tn in range(count):
            bias[b, :, tn * SLOT + TOKENS : (tn + 1) * SLOT, :] = jnp.zeros(
                (2, SLOT - TOKENS, 128), F32
            )
        group = WLAT
        for first in range(0, WZ * WLAT, group):
            rows = spread[first * count : (first + group) * count, :].astype(BF16)
            for w in range(WIDTH):
                picked = mm(rows, pick[:, w * 256 : (w + 1) * 256])
                for g in range(group):
                    n = first + g
                    value = picked[g * count : (g + 1) * count, :] + pad_row
                    if b == 1:
                        forbid = keys_row[1:2, :] if n % WLAT < HALF else keys_row[2:3, :]
                        value = value + jnp.where(late, last * forbid, 0.0)
                    for half in range(2):
                        bias[b, half, pl.ds(w * WZ * WLAT + n, count, stride=SLOT), :] = value[
                            :, half * 128 : (half + 1) * 128
                        ]

    expand(0)

    low = lax.broadcasted_iota(jnp.int32, (SLOT, 128), 1) < 64
    first_half = jnp.where(low, 1.0, 0.0).astype(BF16)
    second_half = jnp.where(low, 0.0, 1.0).astype(BF16)
    scale = (dims // heads) ** -0.5

    def split(value):
        return jnp.concatenate([value * first_half, value * second_half], axis=0)

    def merge(value):
        return jnp.where(low, value[:SLOT], value[SLOT:])

    def lanes(part, pair):
        return pl.ds(pl.multiple_of(part * dims + pair * 128, 128), 128)

    def keys_of(b, rows, part, pair):
        own = qkv[b, rows, lanes(part + 1, pair)]
        other = far[b, rows, lanes(part, pair)]
        return jnp.concatenate([own, other], axis=0)

    def forward(b, t, pair, rows):
        q = split(qkv[b, rows, lanes(0, pair)])
        k = keys_of(b, rows, 0, pair)
        v = keys_of(b, rows, 1, pair)
        at = pl.multiple_of((2 * pair * WINDOWS + t) * SLOT, SLOT)
        parts = []
        for start in (at, pl.multiple_of(at + WINDOWS * SLOT, SLOT)):
            here = pl.ds(start, SLOT)
            row = [bias[b, 0, here, :], bias[b, 1, here, : 2 * SLOT - 128]]
            parts.append(jnp.concatenate(row, axis=1))
        offsets = jnp.concatenate(parts, axis=0)
        scores = mt(q, k) * scale + offsets
        expo = jnp.exp(scores - jnp.max(scores, axis=-1, keepdims=True))
        p = expo * (1.0 / jnp.sum(expo, axis=-1, keepdims=True))
        rounded = p.astype(BF16)
        mixed[rows, lanes(0, pair)] = merge(mm(rounded, v)).astype(BF16)
        return q, k, v, p, rounded

    def backward(b, rows, pair, q, k, v, p, rounded):
        d = split(back[rows, lanes(0, pair)])
        dp = mt(d, v)
        inner = jnp.sum(p * dp, axis=-1, keepdims=True)
        ds = (p * (dp - inner) * scale).astype(BF16)
        grads[rows, lanes(0, pair)] = merge(mm(ds, k)).astype(BF16)
        dk = tm(ds, q).astype(BF16)
        dv = tm(rounded, d).astype(BF16)
        grads[rows, lanes(1, pair)] = dk[:SLOT]
        grads[rows, lanes(2, pair)] = dv[:SLOT]
        far_grads[b, rows, lanes(0, pair)] = dk[SLOT:]
        far_grads[b, rows, lanes(1, pair)] = dv[SLOT:]

    def save_at(t, pair):
        return pl.ds(pl.multiple_of((t * heads + 2 * pair) * SLOT, SLOT), 2 * SLOT)

    def halves(body, b):
        sends = []
        cut = pairs // 2
        for first, last_pair in ((0, cut), (cut, pairs)):
            lax.fori_loop(first, last_pair, body, 0, unroll=True)
            for part in range(2):
                cols = pl.ds(part * dims + first * 128, (last_pair - first) * 128)
                sends.append(
                    send(far_grads.at[b, :, cols], got_grads.at[b, :, cols], partner)
                )
        return sends

    def finish(b, dy, gain, weight, sends):
        dq = grads[:, :dims]
        total = mt(dq, weight[:, :dims])
        arrive(sends)
        for part in (1, 2):
            cols = slice(part * dims, (part + 1) * dims)
            own = grads[:, cols].astype(F32)
            other = got_grads[b, :, (part - 1) * dims : part * dims].astype(F32)
            total = total + mt((own + other).astype(BF16), weight[:, cols])
        scaled = total * gain[...].reshape(1, dims)
        norm = normed[b]
        mean = jnp.mean(scaled, axis=-1, keepdims=True)
        along = jnp.mean(scaled * norm, axis=-1, keepdims=True)
        return (dy + (scaled - mean - norm * along) * inverse[b]).astype(BF16)

    kv_one.wait_recv()

    def one(pair, carry):
        for t in range(WINDOWS):
            rows = pl.ds(t * SLOT, SLOT)
            saved = forward(0, t, pair, rows)
            probs[save_at(t, pair), :] = saved[3]
        return carry

    lax.fori_loop(0, pairs, one, 0, unroll=True)
    loads[2].wait()
    middle = (field[0].astype(F32) + mm(mixed[...], proj_one[...])).astype(BF16)
    moved = roll(1, mm(perms[2], middle), True)
    expand(1)
    arrive(moved)
    field[1] = mm(perms[3], got[1]).astype(BF16)

    kv_two = project(1, gain_two, qkv_two)
    loads[4].wait()
    arrive(cot)
    dy_two = mm(perms[3], got[0])
    back[...] = mt(dy_two.astype(BF16), proj_two[...]).astype(BF16)
    kv_two.wait_recv()

    def two(pair, carry):
        for t in range(WINDOWS):
            rows = pl.ds(t * SLOT, SLOT)
            backward(1, rows, pair, *forward(1, t, pair, rows))
        return carry

    dkv_two = halves(two, 1)
    turned = (field[1].astype(F32) + mm(mixed[...], proj_two[...])).astype(BF16)
    result = roll(2, mm(perms[4], turned), False)
    grad_turned = finish(1, mm(perms[3], got[0]), gain_two, qkv_two, dkv_two)
    moved = roll(3, mm(perms[4], grad_turned), False)
    arrive(result)
    output[...] = mm(perms[6], got[2])[:plain].astype(BF16)
    arrive(moved)

    dy_one = mm(perms[5], got[3])
    back[...] = mt(dy_one.astype(BF16), proj_one[...]).astype(BF16)

    def one_back(pair, carry):
        for t in range(WINDOWS):
            rows = pl.ds(t * SLOT, SLOT)
            q = split(qkv[0, rows, lanes(0, pair)])
            p = probs[save_at(t, pair), :]
            k = keys_of(0, rows, 0, pair)
            v = keys_of(0, rows, 1, pair)
            backward(0, rows, pair, q, k, v, p, p.astype(BF16))
        return carry

    dkv_one = halves(one_back, 0)
    last_grad = finish(0, mm(perms[5], got[3]), gain_one, qkv_one, dkv_one)
    grad_stream[...] = mm(perms[7], last_grad)[:plain].astype(BF16)
    for copy in copies:
        copy.wait_send()


def body(
    lats,
    lons,
    stream,
    land,
    orography,
    land_vector,
    orography_table,
    gain_one,
    qkv_one,
    proj_one,
    table_one,
    gain_two,
    qkv_two,
    proj_two,
    table_two,
    cotangent,
):
    levels, rows, width, dims = stream.shape
    types, heads, entries = table_one.shape
    plain = levels * rows * width
    land_rows, land_cols = land_pickers()
    wide = 3 * dims
    scratch = [
        pltpu.VMEM((2, 2, types * heads * SLOT, 128), F32),
        pltpu.VMEM((WZ * WLAT * types * heads, WZ * 256), F32),
        pltpu.VMEM((types * heads, entries), F32),
        pltpu.VMEM((types * heads * SLOT, 2 * SLOT), F32),
        pltpu.VMEM((2, ROWS, dims), BF16),
        pltpu.VMEM((2, ROWS, dims), F32),
        pltpu.VMEM((2, ROWS, 1), F32),
        pltpu.VMEM((2, ROWS, wide), BF16),
        pltpu.VMEM((2, ROWS, 2 * dims), BF16),
        pltpu.VMEM((ROWS, dims), BF16),
        pltpu.VMEM((ROWS, dims), BF16),
        pltpu.VMEM((ROWS, wide), BF16),
        pltpu.VMEM((2, ROWS, 2 * dims), BF16),
        pltpu.VMEM((2, ROWS, 2 * dims), BF16),
        pltpu.VMEM((4, ROWS, dims), BF16),
        pltpu.VMEM((4, ROWS, dims), BF16),
        pltpu.SemaphoreType.DMA((18,)),
        pltpu.SemaphoreType.DMA((18,)),
        pltpu.VMEM((dims, wide), BF16),
        pltpu.VMEM((dims, dims), BF16),
        pltpu.VMEM((dims, wide), BF16),
        pltpu.VMEM((dims, dims), BF16),
        pltpu.VMEM((WZ * 256, WIDTH * 256), BF16),
        pltpu.SemaphoreType.DMA((5,)),
    ]
    vmem = pl.BlockSpec(memory_space=pltpu.VMEM)
    hbm = pl.BlockSpec(memory_space=pl.ANY)
    out, grad = pl.pallas_call(
        functools.partial(kernel, lats, lons),
        out_shape=[jax.ShapeDtypeStruct((plain, dims), BF16)] * 2,
        in_specs=[vmem] * 6 + [hbm] * 2 + [vmem] + [hbm] * 2 + [vmem] * 4 + [hbm] + [vmem] * 3,
        out_specs=[vmem] * 2,
        scratch_shapes=scratch,
        compiler_params=pltpu.CompilerParams(
            collective_id=0, has_side_effects=True, vmem_limit_bytes=56 << 20
        ),
    )(
        stream.transpose(0, 2, 1, 3).reshape(plain, dims),
        land.T,
        orography.T,
        land_vector,
        orography_table,
        gain_one,
        qkv_one,
        proj_one,
        gain_two,
        qkv_two,
        proj_two,
        table_one.transpose(1, 0, 2),
        table_two.transpose(1, 0, 2),
        cotangent.transpose(0, 2, 1, 3).reshape(plain, dims),
        jnp.asarray(permutations()),
        jnp.asarray(pickers()),
        jnp.asarray(key_rows()),
        jnp.asarray(land_rows),
        jnp.asarray(land_cols),
    )

    def placed(tokens):
        return tokens.reshape(levels, width, rows, dims).transpose(0, 2, 1, 3)

    return placed(out), placed(grad)


def solution(mesh):
    placed = (
        P(None, "lat", "lon", None),
        P("lat", "lon"),
        P("lat", "lon"),
        P(),
        P(),
        P(),
        P(),
        P(),
        P("lat", None, None),
        P(),
        P(),
        P(),
        P("lat", None, None),
        P(None, "lat", "lon", None),
    )
    return jax.shard_map(
        functools.partial(body, mesh.shape["lat"], mesh.shape["lon"]),
        mesh=mesh,
        in_specs=placed,
        out_specs=(P(None, "lat", "lon", None), P(None, "lat", "lon", None)),
        check_vma=False,
    )
```

```python
import functools

import jax
import jax.numpy as jnp
import ml_dtypes
import numpy as np
from jax import lax
from jax.experimental import pallas as pl
from jax.experimental.pallas import tpu as pltpu
from jax.sharding import PartitionSpec as P

WZ = 2
WLAT = 12
WLON = 6
LAND = 16
HALF = WLAT // 2
WIDTH = WLON // 2
WINDOWS = 2
TOKENS = WZ * WLAT * WIDTH
SLOT = 80
ROWS = WINDOWS * SLOT
GROUPS = 3
MAIN = 112
STEP = 2 * WLON - 1
RUN = WLAT * STEP
EPS = 1e-05
F32 = jnp.float32
BF16 = jnp.bfloat16
MESH = pl.DeviceIdType.MESH


def window_place(z, r, w):
    return (r // WLAT) * SLOT + w * WZ * WLAT + z * WLAT + r % WLAT


def plain_place(z, r, w):
    return (z * WIDTH + w) * WINDOWS * WLAT + r


def chunk_place(z, r, w, strip):
    chunk = r // HALF
    inner = (z * HALF + r % HALF) * WIDTH + w
    if chunk == strip:
        return MAIN + inner
    return (chunk if strip else chunk - 1) * WZ * HALF * WIDTH + inner


def permutations():
    out = np.zeros((8, ROWS, ROWS), np.float32)
    rows = WINDOWS * WLAT
    for z in range(WZ):
        for r in range(rows):
            for w in range(WIDTH):
                here = window_place(z, r, w)
                plain = plain_place(z, r, w)
                up = chunk_place(z, r, w, 0)
                down = chunk_place(z, r, w, 3)
                from_up = chunk_place(z, (r + HALF) % rows, w, 0)
                from_down = chunk_place(z, (r - HALF) % rows, w, 3)
                out[0, here, plain] = 1
                out[1, up, plain] = 1
                out[2, up, here] = 1
                out[3, here, from_up] = 1
                out[4, down, here] = 1
                out[5, here, from_down] = 1
                out[6, plain, from_down] = 1
                out[7, plain, here] = 1
    return out.astype(ml_dtypes.bfloat16)


def pickers():
    out = np.zeros((2, WZ * 256, WIDTH * 256), np.float32)
    for p in range(2):
        for w in range(WIDTH):
            for slot in range(2):
                for kw in range(WIDTH):
                    col = WIDTH * (p if slot == 0 else 1 - p) + kw
                    d = WIDTH * p + w - col + WLON - 1
                    for z in range(WZ):
                        for r in range(WLAT):
                            key = slot * SLOT + kw * WZ * WLAT + z * WLAT + r
                            out[p, z * 256 + r * STEP + d, w * 256 + key] = 1
    return out.astype(ml_dtypes.bfloat16)


def key_rows():
    out = np.zeros((8, 256), np.float32)
    for slot in range(2):
        for k in range(SLOT):
            upper = k % WLAT >= HALF
            lane = slot * SLOT + k
            if k >= TOKENS:
                out[0, lane] = -1e30
            else:
                out[1, lane] = -1e9 if upper else 0.0
                out[2, lane] = 0.0 if upper else -1e9
    return out


def land_pickers():
    rows = np.zeros((ROWS, WINDOWS * WLAT), np.float32)
    cols = np.zeros((ROWS, WIDTH), np.float32)
    for z in range(WZ):
        for r in range(WINDOWS * WLAT):
            for w in range(WIDTH):
                here = window_place(z, r, w)
                rows[here, r] = 1
                cols[here, w] = 1
    return rows.astype(ml_dtypes.bfloat16), cols


def mm(a, b):
    return lax.dot_general(a, b, (((1,), (0,)), ((), ())), preferred_element_type=F32)


def mt(a, b):
    return lax.dot_general(a, b, (((1,), (1,)), ((), ())), preferred_element_type=F32)


def tm(a, b):
    return lax.dot_general(a, b, (((0,), (0,)), ((), ())), preferred_element_type=F32)


def kernel(
    lats,
    lons,
    stream,
    land,
    orography,
    land_vector,
    orography_table,
    gain_one,
    hbm_qkv_one,
    hbm_proj_one,
    gain_two,
    hbm_qkv_two,
    hbm_proj_two,
    hbm_table_one,
    hbm_table_two,
    hbm_cotangent,
    perms,
    hbm_picks,
    keys_row,
    land_rows,
    land_cols,
    output,
    grad_stream,
    bias,
    spread,
    entries,
    probs,
    field,
    normed,
    inverse,
    qkv,
    far,
    mixed,
    back,
    grads,
    far_grads,
    got_grads,
    sent,
    got,
    send_sem,
    recv_sem,
    qkv_one,
    proj_one,
    qkv_two,
    proj_two,
    pick,
    table_one,
    table_two,
    cotangent,
    load_sem,
):
    dims = stream.shape[1]
    heads = table_one.shape[0]
    tables = (table_one, table_two)
    pairs = heads // 2
    i = lax.axis_index("lat")
    j = lax.axis_index("lon")
    parity = lax.rem(j, 2)
    next_lat = lax.rem(i + 1, lats)
    prev_lat = lax.rem(i + lats - 1, lats)
    east = lax.rem(j + 1, lons)
    west = lax.rem(j + lons - 1, lons)
    partner = (i, j + 1 - 2 * parity)

    loads = []
    for source, target in (
        (hbm_qkv_one, qkv_one),
        (hbm_picks.at[parity], pick),
        (hbm_cotangent, cotangent),
        (hbm_table_one, table_one),
        (hbm_table_two, table_two),
        (hbm_proj_one, proj_one),
        (hbm_qkv_two, qkv_two),
        (hbm_proj_two, proj_two),
    ):
        load = pltpu.make_async_copy(source, target, load_sem.at[len(loads)])
        load.start()
        loads.append(load)

    barrier = pltpu.get_barrier_semaphore()
    for peer in ((i, east), (i, west), (next_lat, east), (prev_lat, west)):
        pl.semaphore_signal(barrier, inc=1, device_id=peer, device_id_type=MESH)

    copies = []

    def send(src, dst, to):
        n = len(copies)
        copy = pltpu.make_async_remote_copy(
            src_ref=src,
            dst_ref=dst,
            send_sem=send_sem.at[n],
            recv_sem=recv_sem.at[n],
            device_id=to,
            device_id_type=MESH,
        )
        copy.start()
        copies.append(copy)
        return copy

    def roll(slot, moved, up):
        sent[slot] = moved.astype(BF16)
        main = (i, west) if up else (i, east)
        strip = (prev_lat, west) if up else (next_lat, east)
        a = send(sent.at[slot, pl.ds(0, MAIN)], got.at[slot, pl.ds(0, MAIN)], main)
        rest = pl.ds(MAIN, ROWS - MAIN)
        b = send(sent.at[slot, rest], got.at[slot, rest], strip)
        return a, b

    def arrive(both):
        for copy in both:
            copy.wait_recv()

    plain = WZ * WINDOWS * WLAT * WIDTH

    row_pick = land_rows[...]
    col_pick = land_cols[...]

    def per_token(ref):
        spread_rows = mt(row_pick, ref[...].astype(F32).astype(BF16))
        return jnp.sum(spread_rows * col_pick, axis=1, keepdims=True)

    classes = per_token(orography)
    added = (per_token(land) * (1.0 / LAND)) * land_vector[...].reshape(1, dims)
    for k in range(orography_table.shape[0]):
        added = added + jnp.where(classes == float(k), 1.0, 0.0) * orography_table[k : k + 1, :]
    embedded = (mm(perms[0, :, :plain], stream[...]) + added).astype(BF16)
    field[0] = embedded

    def project(b, gain, weight):
        values = field[b].astype(F32)
        centred = values - jnp.mean(values, axis=-1, keepdims=True)
        inv = lax.rsqrt(jnp.mean(centred * centred, axis=-1, keepdims=True) + EPS)
        norm = centred * inv
        normed[b] = norm
        inverse[b] = inv
        h = (norm * gain[...].reshape(1, dims)).astype(BF16)
        loads[0 if b == 0 else 6].wait()
        for part in (1, 2):
            cols = slice(part * dims, (part + 1) * dims)
            qkv[b, :, cols] = mm(h, weight[:, cols]).astype(BF16)
        if b == 0:
            pl.semaphore_wait(barrier, 4)
        copy = send(qkv.at[b, :, pl.ds(dims, 2 * dims)], far.at[b], partner)
        qkv[b, :, :dims] = mm(h, weight[:, :dims]).astype(BF16)
        return copy

    kv_one = project(0, gain_one, qkv_one)
    loads[2].wait()
    cot = roll(0, mm(perms[1, :, :plain], cotangent[...]), True)

    loads[1].wait()
    last = jnp.where(i == lats - 1, 1.0, 0.0).astype(F32)
    pad_row = keys_row[0:1, :]
    count = WINDOWS * heads
    late = lax.broadcasted_iota(jnp.int32, (count, 256), 0) % WINDOWS == WINDOWS - 1

    def expand(b):
        loads[3 + b].wait()
        for n in range(heads):
            entries[n * WINDOWS : (n + 1) * WINDOWS, :] = tables[b][n].astype(F32)
        for za in range(WZ):
            for ra in range(WLAT):
                n = za * WLAT + ra
                for zc in range(WZ):
                    k = (za * WZ + zc) * WLAT + ra
                    stop = min(RUN * k + 256, entries.shape[1])
                    run = entries[:, RUN * k : stop]
                    if run.shape[1] < 256:
                        rest = jnp.zeros((count, 256 - run.shape[1]), F32)
                        run = jnp.concatenate([run, rest], axis=1)
                    spread[n * count : (n + 1) * count, zc * 256 : (zc + 1) * 256] = run
        for tn in range(count):
            bias[b, :, tn * SLOT + TOKENS : (tn + 1) * SLOT, :] = jnp.zeros(
                (2, SLOT - TOKENS, 128), F32
            )
        group = WLAT
        for first in range(0, WZ * WLAT, group):
            rows = spread[first * count : (first + group) * count, :].astype(BF16)
            for w in range(WIDTH):
                picked = mm(rows, pick[:, w * 256 : (w + 1) * 256])
                for g in range(group):
                    n = first + g
                    value = picked[g * count : (g + 1) * count, :] + pad_row
                    if b == 1:
                        forbid = keys_row[1:2, :] if n % WLAT < HALF else keys_row[2:3, :]
                        value = value + jnp.where(late, last * forbid, 0.0)
                    for half in range(2):
                        bias[b, half, pl.ds(w * WZ * WLAT + n, count, stride=SLOT), :] = value[
                            :, half * 128 : (half + 1) * 128
                        ]

    expand(0)

    low = lax.broadcasted_iota(jnp.int32, (SLOT, 128), 1) < 64
    first_half = jnp.where(low, 1.0, 0.0).astype(BF16)
    second_half = jnp.where(low, 0.0, 1.0).astype(BF16)
    scale = (dims // heads) ** -0.5

    def split(value):
        return jnp.concatenate([value * first_half, value * second_half], axis=0)

    def merge(value):
        return jnp.where(low, value[:SLOT], value[SLOT:])

    def lanes(part, pair):
        return pl.ds(pl.multiple_of(part * dims + pair * 128, 128), 128)

    def keys_of(b, rows, part, pair):
        own = qkv[b, rows, lanes(part + 1, pair)]
        other = far[b, rows, lanes(part, pair)]
        return jnp.concatenate([own, other], axis=0)

    def forward(b, t, pair, rows):
        q = split(qkv[b, rows, lanes(0, pair)])
        k = keys_of(b, rows, 0, pair)
        v = keys_of(b, rows, 1, pair)
        at = pl.multiple_of((2 * pair * WINDOWS + t) * SLOT, SLOT)
        parts = []
        for start in (at, pl.multiple_of(at + WINDOWS * SLOT, SLOT)):
            here = pl.ds(start, SLOT)
            row = [bias[b, 0, here, :], bias[b, 1, here, : 2 * SLOT - 128]]
            parts.append(jnp.concatenate(row, axis=1))
        offsets = jnp.concatenate(parts, axis=0)
        scores = mt(q, k) * scale + offsets
        expo = jnp.exp(scores - jnp.max(scores, axis=-1, keepdims=True))
        p = expo * (1.0 / jnp.sum(expo, axis=-1, keepdims=True))
        rounded = p.astype(BF16)
        mixed[rows, lanes(0, pair)] = merge(mm(rounded, v)).astype(BF16)
        return q, k, v, p, rounded

    def backward(b, rows, pair, q, k, v, p, rounded):
        d = split(back[rows, lanes(0, pair)])
        dp = mt(d, v)
        inner = jnp.sum(p * dp, axis=-1, keepdims=True)
        ds = (p * (dp - inner) * scale).astype(BF16)
        grads[rows, lanes(0, pair)] = merge(mm(ds, k)).astype(BF16)
        dk = tm(ds, q).astype(BF16)
        dv = tm(rounded, d).astype(BF16)
        grads[rows, lanes(1, pair)] = dk[:SLOT]
        grads[rows, lanes(2, pair)] = dv[:SLOT]
        far_grads[b, rows, lanes(0, pair)] = dk[SLOT:]
        far_grads[b, rows, lanes(1, pair)] = dv[SLOT:]

    def save_at(t, pair):
        return pl.ds(pl.multiple_of((t * heads + 2 * pair) * SLOT, SLOT), 2 * SLOT)

    def grouped(body, b):
        sends = []
        step = pairs // GROUPS
        for first in range(0, pairs, step):
            last_pair = first + step
            lax.fori_loop(first, last_pair, body, 0, unroll=True)
            for part in range(2):
                cols = pl.ds(part * dims + first * 128, (last_pair - first) * 128)
                sends.append(
                    send(far_grads.at[b, :, cols], got_grads.at[b, :, cols], partner)
                )
        return sends

    def finish(b, dy, gain, weight, sends):
        dq = grads[:, :dims]
        total = mt(dq, weight[:, :dims])
        arrive(sends)
        for part in (1, 2):
            cols = slice(part * dims, (part + 1) * dims)
            own = grads[:, cols].astype(F32)
            other = got_grads[b, :, (part - 1) * dims : part * dims].astype(F32)
            total = total + mt((own + other).astype(BF16), weight[:, cols])
        scaled = total * gain[...].reshape(1, dims)
        norm = normed[b]
        mean = jnp.mean(scaled, axis=-1, keepdims=True)
        along = jnp.mean(scaled * norm, axis=-1, keepdims=True)
        return (dy + (scaled - mean - norm * along) * inverse[b]).astype(BF16)

    kv_one.wait_recv()

    def one(pair, carry):
        for t in range(WINDOWS):
            rows = pl.ds(t * SLOT, SLOT)
            saved = forward(0, t, pair, rows)
            probs[save_at(t, pair), :] = saved[3]
        return carry

    lax.fori_loop(0, pairs, one, 0, unroll=True)
    loads[5].wait()
    middle = (field[0].astype(F32) + mm(mixed[...], proj_one[...])).astype(BF16)
    moved = roll(1, mm(perms[2], middle), True)
    expand(1)
    arrive(moved)
    field[1] = mm(perms[3], got[1]).astype(BF16)

    kv_two = project(1, gain_two, qkv_two)
    loads[7].wait()
    arrive(cot)
    dy_two = mm(perms[3], got[0])
    back[...] = mt(dy_two.astype(BF16), proj_two[...]).astype(BF16)
    kv_two.wait_recv()

    def two(pair, carry):
        for t in range(WINDOWS):
            rows = pl.ds(t * SLOT, SLOT)
            backward(1, rows, pair, *forward(1, t, pair, rows))
        return carry

    dkv_two = grouped(two, 1)
    grad_turned = finish(1, mm(perms[3], got[0]), gain_two, qkv_two, dkv_two)
    moved = roll(3, mm(perms[4], grad_turned), False)
    turned = (field[1].astype(F32) + mm(mixed[...], proj_two[...])).astype(BF16)
    result = roll(2, mm(perms[4], turned), False)
    arrive(moved)

    dy_one = mm(perms[5], got[3])
    back[...] = mt(dy_one.astype(BF16), proj_one[...]).astype(BF16)

    def one_back(pair, carry):
        for t in range(WINDOWS):
            rows = pl.ds(t * SLOT, SLOT)
            q = split(qkv[0, rows, lanes(0, pair)])
            p = probs[save_at(t, pair), :]
            k = keys_of(0, rows, 0, pair)
            v = keys_of(0, rows, 1, pair)
            backward(0, rows, pair, q, k, v, p, p.astype(BF16))
        return carry

    dkv_one = grouped(one_back, 0)
    arrive(result)
    output[...] = mm(perms[6], got[2])[:plain].astype(BF16)
    last_grad = finish(0, mm(perms[5], got[3]), gain_one, qkv_one, dkv_one)
    grad_stream[...] = mm(perms[7], last_grad)[:plain].astype(BF16)
    for copy in copies:
        copy.wait_send()


def hand_over(first, second, first_out, second_out, sem):
    copies = []
    for source, target in ((first, first_out), (second, second_out)):
        step = source.shape[0] // 3
        for n in range(3):
            rows = pl.ds(n * step, step)
            copies.append(
                pltpu.make_async_copy(source.at[rows], target.at[rows], sem.at[len(copies)])
            )
    for copy in copies:
        copy.start()
    for copy in copies:
        copy.wait()


def body(
    lats,
    lons,
    stream,
    land,
    orography,
    land_vector,
    orography_table,
    gain_one,
    qkv_one,
    proj_one,
    table_one,
    gain_two,
    qkv_two,
    proj_two,
    table_two,
    cotangent,
):
    levels, rows, width, dims = stream.shape
    types, heads, entries = table_one.shape
    plain = levels * rows * width
    land_rows, land_cols = land_pickers()
    wide = 3 * dims
    scratch = [
        pltpu.VMEM((2, 2, types * heads * SLOT, 128), F32),
        pltpu.VMEM((WZ * WLAT * types * heads, WZ * 256), F32),
        pltpu.VMEM((types * heads, entries), F32),
        pltpu.VMEM((types * heads * SLOT, 2 * SLOT), F32),
        pltpu.VMEM((2, ROWS, dims), BF16),
        pltpu.VMEM((2, ROWS, dims), F32),
        pltpu.VMEM((2, ROWS, 1), F32),
        pltpu.VMEM((2, ROWS, wide), BF16),
        pltpu.VMEM((2, ROWS, 2 * dims), BF16),
        pltpu.VMEM((ROWS, dims), BF16),
        pltpu.VMEM((ROWS, dims), BF16),
        pltpu.VMEM((ROWS, wide), BF16),
        pltpu.VMEM((2, ROWS, 2 * dims), BF16),
        pltpu.VMEM((2, ROWS, 2 * dims), BF16),
        pltpu.VMEM((4, ROWS, dims), BF16),
        pltpu.VMEM((4, ROWS, dims), BF16),
        pltpu.SemaphoreType.DMA((22,)),
        pltpu.SemaphoreType.DMA((22,)),
        pltpu.VMEM((dims, wide), BF16),
        pltpu.VMEM((dims, dims), BF16),
        pltpu.VMEM((dims, wide), BF16),
        pltpu.VMEM((dims, dims), BF16),
        pltpu.VMEM((WZ * 256, WIDTH * 256), BF16),
        pltpu.VMEM((heads, types, entries), BF16),
        pltpu.VMEM((heads, types, entries), BF16),
        pltpu.VMEM((plain, dims), BF16),
        pltpu.SemaphoreType.DMA((8,)),
    ]
    vmem = pl.BlockSpec(memory_space=pltpu.VMEM)
    hbm = pl.BlockSpec(memory_space=pl.ANY)
    out, grad = pl.pallas_call(
        functools.partial(kernel, lats, lons),
        out_shape=[jax.ShapeDtypeStruct((plain, dims), BF16)] * 2,
        in_specs=[vmem] * 6 + [hbm] * 2 + [vmem] + [hbm] * 5 + [vmem] + [hbm] + [vmem] * 3,
        out_specs=[vmem] * 2,
        scratch_shapes=scratch,
        compiler_params=pltpu.CompilerParams(
            collective_id=0, has_side_effects=True, vmem_limit_bytes=56 << 20
        ),
    )(
        stream.transpose(0, 2, 1, 3).reshape(plain, dims),
        land.T,
        orography.T,
        land_vector,
        orography_table,
        gain_one,
        qkv_one,
        proj_one,
        gain_two,
        qkv_two,
        proj_two,
        table_one.transpose(1, 0, 2),
        table_two.transpose(1, 0, 2),
        cotangent.transpose(0, 2, 1, 3).reshape(plain, dims),
        jnp.asarray(permutations()),
        jnp.asarray(pickers()),
        jnp.asarray(key_rows()),
        jnp.asarray(land_rows),
        jnp.asarray(land_cols),
    )

    out, grad = pl.pallas_call(
        hand_over,
        out_shape=[jax.ShapeDtypeStruct((plain, dims), BF16)] * 2,
        in_specs=[hbm] * 2,
        out_specs=[hbm] * 2,
        scratch_shapes=[pltpu.SemaphoreType.DMA((6,))],
        compiler_params=pltpu.CompilerParams(vmem_limit_bytes=62 << 20),
    )(out, grad)

    def placed(tokens):
        return tokens.reshape(levels, width, rows, dims).transpose(0, 2, 1, 3)

    return placed(out), placed(grad)


def solution(mesh):
    placed = (
        P(None, "lat", "lon", None),
        P("lat", "lon"),
        P("lat", "lon"),
        P(),
        P(),
        P(),
        P(),
        P(),
        P("lat", None, None),
        P(),
        P(),
        P(),
        P("lat", None, None),
        P(None, "lat", "lon", None),
    )
    return jax.shard_map(
        functools.partial(body, mesh.shape["lat"], mesh.shape["lon"]),
        mesh=mesh,
        in_specs=placed,
        out_specs=(P(None, "lat", "lon", None), P(None, "lat", "lon", None)),
        check_vma=False,
    )
```
